32 devices in a mesh: dp: 8 (over y, x, core), tensor: 4 (over z).
Axes of the slice: x: 2, y: 2, z: 4, core: 2. Of those that a mesh axis runs over, the one named last changes fastest.
Arguments:
- gradients: bfloat16 [8, 8192, 1024], P('dp', 'tensor'), may hold values from -8 to 8
- errors: bfloat16 [8, 8192, 1024], P('dp', 'tensor'), may hold values from -3 to 3
- right_factors: float32 [32, 1024], replicated, may hold values from -6 to 6
Outputs:
- new_errors: bfloat16 [8, 8192, 1024], P('dp', 'tensor')
- new_factors: float32 [32, 1024], replicated
- update: bfloat16 [8192, 1024], P('tensor')
The draws below stay inside these ranges and needn't reach their ends.
All inputs are finite; a program needn't handle non-finite values.
Results may differ from the reference program's by a relative error of at most 0.001.
Values sent between devices are 32-bit elements; how exact they have to be, the bound alone decides.
A program may use at most 64 MiB of HBM per device.

```python
import jax
import jax.numpy as jnp
from jax import lax

D = 8192
KV = 1024
R = 32
REPLICAS = 8
N_DP = 8


def draw_gradients(key, part):
    key = jax.random.fold_in(key, 11)
    key_common, key_rows, key_cols, key_own = jax.random.split(key, 4)
    common = jax.random.normal(key_common, (D, KV), jnp.float32)
    row_scale = jnp.exp(jax.random.uniform(key_rows, (D, 1), jnp.float32, jnp.log(0.3), jnp.log(3.0)))
    col_scale = jnp.exp(jax.random.uniform(key_cols, (1, KV), jnp.float32, jnp.log(0.3), jnp.log(3.0)))
    own_part = 0.5 * jax.random.normal(key_own, (N_DP, D, KV), jnp.float32)
    values = (common * row_scale * col_scale)[None] + own_part
    return jnp.clip(values, -8.0, 8.0).astype(jnp.bfloat16)


def steps_of(stream_key, extent, pieces, low, largest):
    loudness, own = 1.0, jax.random.fold_in(stream_key, 6)
    for axis_at, blocks in pieces:
        draws = jnp.exp(jax.random.uniform(jax.random.fold_in(own, axis_at), (blocks,), jnp.float32, low / len(pieces), largest / len(pieces)))
        loudness = loudness * jnp.repeat(draws, extent[axis_at] // blocks).reshape([-1 if axis == axis_at else 1 for axis in range(len(extent))])
    return loudness


def noise(rng, extent, deviation, limit, shards=(), held_as=jnp.bfloat16):
    gain = steps_of(rng, extent, shards, -0.22, 0.18) if shards else 1.0
    entries = jax.random.normal(rng, extent, jnp.float32) * deviation * gain
    return jnp.minimum(jnp.maximum(entries, -limit), limit).astype(held_as)


def setup_inputs(seed: int = 0) -> dict:
    key_list = jax.random.split(jax.random.key(seed), 4)
    return {
        "gradients": draw_gradients(jax.random.fold_in(key_list[3], 71), 0),
        "errors": noise(key_list[1], (REPLICAS, D, KV), 0.5, 3.0, ((0, 8), (1, 4))),
        "right_factors": noise(key_list[2], (R, KV), 1.0, 6.0, (), jnp.float32),
    }


def reference(gradients, errors, right_factors):
    highest = lax.Precision.HIGHEST

    def p_term(carry, inputs_pair):
        merged = inputs_pair[0].astype(jnp.float32) + inputs_pair[1].astype(jnp.float32)
        product = lax.dot_general(right_factors, merged, (((1,), (1,)), ((), ())), precision=highest)
        return (carry + product, None)
    p_summed, unused = lax.scan(p_term, jnp.zeros((R, D), jnp.float32), (gradients, errors))
    p_rows = p_summed / N_DP
    gram_matrix = jnp.dot(p_rows, p_rows.T, precision=highest)
    lower_factor = lax.linalg.cholesky(gram_matrix)
    ortho_rows = lax.linalg.triangular_solve(lower_factor, p_rows, left_side=True, lower=True)

    def q_term(carry, inputs_pair):
        merged = inputs_pair[0].astype(jnp.float32) + inputs_pair[1].astype(jnp.float32)
        return (carry + jnp.dot(ortho_rows, merged, precision=highest), None)
    q_summed, unused = lax.scan(q_term, jnp.zeros((R, KV), jnp.float32), (gradients, errors))
    new_factors = q_summed / N_DP
    approx = lax.dot_general(ortho_rows, new_factors, (((0,), (0,)), ((), ())), precision=highest)

    def error_term(inputs_pair):
        merged = inputs_pair[0].astype(jnp.float32) + inputs_pair[1].astype(jnp.float32)
        return (merged - approx).astype(jnp.bfloat16)
    new_errors = lax.map(error_term, (gradients, errors))
    return (new_errors, new_factors, approx.astype(jnp.bfloat16))
```

```python
import functools

import jax
import jax.numpy as jnp
from jax import lax
from jax.experimental import pallas as pl
from jax.experimental.pallas import tpu as pltpu
from jax.sharding import PartitionSpec as P

MESH = pl.DeviceIdType.MESH
F32 = jnp.float32
BF16 = jnp.bfloat16
HIGHEST = lax.Precision.HIGHEST


def split3(x):
    hi = x.astype(BF16)
    rest = x - hi.astype(F32)
    mid = rest.astype(BF16)
    low = (rest - mid.astype(F32)).astype(BF16)
    return hi, mid, low


def inverse_factor(gram, rank):
    rows = lax.broadcasted_iota(jnp.int32, (rank, 128), 0)
    lanes = lax.broadcasted_iota(jnp.int32, (rank, 128), 1)
    both = jnp.where(lanes == rows + rank, 1.0, gram)
    scale = jnp.ones((rank, 128), F32)
    for k in range(rank):
        column = jnp.broadcast_to(both[:, k : k + 1], (rank, 128))
        pivot = column[k : k + 1, :]
        scale = jnp.where(rows == k, pivot, scale)
        factor = jnp.where(rows > k, column * (1.0 / pivot), 0.0)
        both = both - factor * both[k : k + 1, :]
    both = both / jnp.sqrt(scale)
    return both[:, rank : 2 * rank]


def reduce_kernel(
    n_dp, n_t, own_p, own_s,
    g_hbm, e_hbm, r_hbm, ortho_ref, q_ref,
    g_v, e_v, r_v, p_loc, p_in, p_full, s_acc, s_loc, s_in, z_in, q_full,
    gram_k, gram_in,
    g_sem, e_sem, r_sem,
    ps_send, ps_recv, pg_send, pg_recv, gr_send, gr_recv,
    ss_send, ss_recv, z_send, z_recv, q_send, q_recv,
):
    me = lax.axis_index("dp")
    mt = lax.axis_index("tensor")
    rank = r_v.shape[0]
    width = g_v.shape[1]
    cols = s_loc.shape[2]

    def peer(k):
        return lax.rem(me + k, n_dp)

    def tpeer(k):
        return lax.rem(mt + k, n_t)

    def chunk(d):
        return lax.rem(me + d, own_p)

    def remote(src, dst, send, recv, dp, t):
        return pltpu.make_async_remote_copy(
            src_ref=src, dst_ref=dst, send_sem=send, recv_sem=recv,
            device_id=(dp, t), device_id_type=MESH,
        )

    def guard(condition, always):
        if always:
            return lambda f: f()
        return pl.when(condition)

    def load(c):
        return (
            pltpu.make_async_copy(g_hbm.at[0, pl.ds(c * width, width)], g_v.at[c], g_sem.at[c]),
            pltpu.make_async_copy(e_hbm.at[0, pl.ds(c * width, width)], e_v.at[c], e_sem.at[c]),
        )

    r_copy = pltpu.make_async_copy(r_hbm, r_v, r_sem)
    r_copy.start()
    for d in range(1, own_p + 1):
        for copy in load(chunk(d)):
            copy.start()

    gram_k[...] = jnp.zeros_like(gram_k)
    barrier = pltpu.get_barrier_semaphore()
    for k in range(1, n_dp):
        pl.semaphore_signal(barrier, inc=1, device_id=(peer(k), mt), device_id_type=MESH)
    for k in range(1, n_t):
        pl.semaphore_signal(barrier, inc=1, device_id=(me, tpeer(k)), device_id_type=MESH)

    r_copy.wait()
    r3 = jnp.concatenate(split3(r_v[...]), axis=0)
    pl.semaphore_wait(barrier, n_dp - 1 + n_t - 1)

    def fold(x):
        return x[:rank] + x[rank : 2 * rank] + x[2 * rank :]

    nt = (((1,), (1,)), ((), ()))

    for d in range(1, own_p + 1):
        c = chunk(d)
        for copy in load(c):
            copy.wait()
        both = lax.dot_general(r3, g_v[c], nt, preferred_element_type=F32)
        both += lax.dot_general(r3, e_v[c], nt, preferred_element_type=F32)
        p_loc[c] = fold(both)
        if not (own_p == n_dp and d == own_p):
            @guard(c != me, own_p == n_dp)
            def _():
                remote(p_loc.at[c], p_in.at[me], ps_send.at[c], ps_recv.at[me], c, mt).start()

    is_p = me < own_p

    @guard(is_p, own_p == n_dp)
    def _():
        total = p_loc[me]
        for k in range(1, n_dp):
            o = peer(k)
            remote(p_loc.at[0], p_in.at[o], ps_send.at[0], ps_recv.at[o], o, mt).wait_recv()
            total = total + p_in[o]
        p_full[me] = total / n_dp
        for k in range(1, n_dp):
            o = peer(k)
            remote(p_full.at[me], p_full.at[me], pg_send.at[o], pg_recv.at[me], o, mt).start()

    for d in range(own_p):
        c = chunk(d)
        if not (own_p == n_dp and d == 0):
            @guard(c != me, own_p == n_dp)
            def _():
                remote(p_full.at[c], p_full.at[c], pg_send.at[0], pg_recv.at[c], c, mt).wait_recv()
        p = p_full[c]
        gram_k[c, :, :rank] = lax.dot_general(p, p, nt, precision=HIGHEST, preferred_element_type=F32)
        if d == own_p - 1:
            gram = gram_k[0]
            for k in range(1, own_p):
                gram = gram + gram_k[k]
            gram_in[mt] = gram
            for k in range(1, n_t):
                o = tpeer(k)
                remote(gram_in.at[mt], gram_in.at[mt], gr_send.at[o], gr_recv.at[mt], me, o).start()
        p3 = jnp.concatenate(split3(p), axis=0)
        both = jnp.dot(p3, g_v[c], preferred_element_type=F32)
        both += jnp.dot(p3, e_v[c], preferred_element_type=F32)
        if d == 0:
            s_acc[...] = fold(both)
        else:
            s_acc[...] += fold(both)

    for j in range(own_s):
        s_loc[j] = s_acc[:, j * cols : (j + 1) * cols]
    for d in range(1, own_s + 1):
        j = lax.rem(me + d, own_s)
        if not (own_s == n_dp and d == own_s):
            @guard(j != me, own_s == n_dp)
            def _():
                remote(s_loc.at[j], s_in.at[me], ss_send.at[j], ss_recv.at[me], j, mt).start()

    for k in range(1, n_t):
        o = tpeer(k)
        remote(gram_in.at[o], gram_in.at[o], gr_send.at[0], gr_recv.at[o], me, o).wait_recv()
    gram = gram_in[0]
    for k in range(1, n_t):
        gram = gram + gram_in[k]
    lanes = lax.broadcasted_iota(jnp.int32, (rank, 128), 1)
    gram = jnp.where(lanes < rank, gram, 0.0)
    is_s = me < own_s

    def share_sum():
        total = s_loc[me]
        for k in range(1, n_dp):
            o = peer(k)
            remote(s_loc.at[0], s_in.at[o], ss_send.at[0], ss_recv.at[o], o, mt).wait_recv()
            total = total + s_in[o]
        z_in[mt] = total
        for k in range(1, n_t):
            o = tpeer(k)
            remote(z_in.at[mt], z_in.at[mt], z_send.at[o], z_recv.at[mt], me, o).start()

    guard(is_s, own_s == n_dp)(share_sum)
    inverse = inverse_factor(gram, rank)

    @guard(is_s, own_s == n_dp)
    def _():
        for k in range(1, n_t):
            o = tpeer(k)
            remote(z_in.at[o], z_in.at[o], z_send.at[0], z_recv.at[o], me, o).wait_recv()
        total = z_in[0]
        for k in range(1, n_t):
            total = total + z_in[k]
        q_full[me] = jnp.dot(inverse, total / n_dp, precision=HIGHEST, preferred_element_type=F32)
        for k in range(1, n_dp):
            o = peer(k)
            remote(q_full.at[me], q_full.at[me], q_send.at[o], q_recv.at[me], o, mt).start()

    for c in range(own_p):
        ortho_ref[:, c * width : (c + 1) * width] = jnp.dot(
            inverse, p_full[c], precision=HIGHEST, preferred_element_type=F32
        )

    for d in range(1, own_s + 1):
        j = lax.rem(me + d, own_s)
        if not (own_s == n_dp and d == own_s):
            @guard(j != me, own_s == n_dp)
            def _():
                remote(q_full.at[j], q_full.at[j], q_send.at[0], q_recv.at[j], j, mt).wait_recv()
    for j in range(own_s):
        q_ref[:, j * cols : (j + 1) * cols] = q_full[j]

    for d in range(1, own_p + 1):
        c = chunk(d)
        if not (own_p == n_dp and d == own_p):
            @guard(c != me, own_p == n_dp)
            def _():
                remote(p_loc.at[c], p_in.at[me], ps_send.at[c], ps_recv.at[me], c, mt).wait_send()
    for d in range(1, own_s + 1):
        j = lax.rem(me + d, own_s)
        if not (own_s == n_dp and d == own_s):
            @guard(j != me, own_s == n_dp)
            def _():
                remote(s_loc.at[j], s_in.at[me], ss_send.at[j], ss_recv.at[me], j, mt).wait_send()
    for k in range(1, n_t):
        o = tpeer(k)
        remote(gram_in.at[mt], gram_in.at[mt], gr_send.at[o], gr_recv.at[mt], me, o).wait_send()

    @guard(is_p, own_p == n_dp)
    def _():
        for k in range(1, n_dp):
            o = peer(k)
            remote(p_full.at[me], p_full.at[me], pg_send.at[o], pg_recv.at[me], o, mt).wait_send()

    @guard(is_s, own_s == n_dp)
    def _():
        for k in range(1, n_dp):
            o = peer(k)
            remote(q_full.at[me], q_full.at[me], q_send.at[o], q_recv.at[me], o, mt).wait_send()
        for k in range(1, n_t):
            o = tpeer(k)
            remote(z_in.at[mt], z_in.at[mt], z_send.at[o], z_recv.at[mt], me, o).wait_send()


def apply_kernel(g_ref, e_ref, ortho_ref, q_ref, err_ref, factors_ref, update_ref, q6_ref):
    @pl.when(pl.program_id(0) == 0)
    def _():
        q = q_ref[...]
        factors_ref[...] = q
        hi, mid, low = split3(q)
        q6_ref[...] = jnp.concatenate([hi, mid, hi, low, mid, hi], axis=0)

    hi, mid, low = split3(ortho_ref[...])
    left = jnp.concatenate([hi, hi, mid, hi, mid, low], axis=0)
    approx = lax.dot_general(
        left, q6_ref[...], (((0,), (0,)), ((), ())), preferred_element_type=F32
    )
    update_ref[...] = approx.astype(BF16)
    err_ref[0] = ((g_ref[0].astype(F32) + e_ref[0].astype(F32)) - approx).astype(BF16)


def per_device(gradients, errors, right_factors):
    n_dp, n_t = lax.axis_size("dp"), lax.axis_size("tensor")
    rows, kv = gradients.shape[1:]
    rank = right_factors.shape[0]
    own_p = min(n_dp, rows // 128)
    own_s = min(n_dp, kv // 128)
    width, cols = rows // own_p, kv // own_s
    dma = pltpu.SemaphoreType.DMA
    ortho, q = pl.pallas_call(
        functools.partial(reduce_kernel, n_dp, n_t, own_p, own_s),
        out_shape=(
            jax.ShapeDtypeStruct((rank, rows), F32),
            jax.ShapeDtypeStruct((rank, kv), F32),
        ),
        in_specs=[pl.BlockSpec(memory_space=pl.ANY)] * 3,
        out_specs=(pl.BlockSpec(memory_space=pltpu.VMEM),) * 2,
        scratch_shapes=[
            pltpu.VMEM((own_p, width, kv), BF16),
            pltpu.VMEM((own_p, width, kv), BF16),
            pltpu.VMEM((rank, kv), F32),
            pltpu.VMEM((own_p, rank, width), F32),
            pltpu.VMEM((n_dp, rank, width), F32),
            pltpu.VMEM((own_p, rank, width), F32),
            pltpu.VMEM((rank, kv), F32),
            pltpu.VMEM((own_s, rank, cols), F32),
            pltpu.VMEM((n_dp, rank, cols), F32),
            pltpu.VMEM((n_t, rank, cols), F32),
            pltpu.VMEM((own_s, rank, cols), F32),
            pltpu.VMEM((own_p, rank, 128), F32),
            pltpu.VMEM((n_t, rank, 128), F32),
            dma((own_p,)), dma((own_p,)), dma,
            dma((own_p,)), dma((n_dp,)), dma((n_dp,)), dma((own_p,)),
            dma((n_t,)), dma((n_t,)),
            dma((own_s,)), dma((n_dp,)), dma((n_t,)), dma((n_t,)),
            dma((n_dp,)), dma((own_s,)),
        ],
        compiler_params=pltpu.CompilerParams(
            collective_id=0, has_side_effects=True, vmem_limit_bytes=40 * 2**20
        ),
    )(gradients, errors, right_factors)

    block = min(256, rows)
    big = pl.BlockSpec((1, block, kv), lambda i: (0, i, 0))
    return pl.pallas_call(
        apply_kernel,
        grid=(rows // block,),
        out_shape=(
            jax.ShapeDtypeStruct((1, rows, kv), BF16),
            jax.ShapeDtypeStruct((rank, kv), F32),
            jax.ShapeDtypeStruct((rows, kv), BF16),
        ),
        in_specs=[
            big, big,
            pl.BlockSpec((rank, block), lambda i: (0, i)),
            pl.BlockSpec((rank, kv), lambda i: (0, 0)),
        ],
        out_specs=(
            big,
            pl.BlockSpec((rank, kv), lambda i: (0, 0)),
            pl.BlockSpec((block, kv), lambda i: (i, 0)),
        ),
        scratch_shapes=[pltpu.VMEM((6 * rank, kv), BF16)],
        compiler_params=pltpu.CompilerParams(vmem_limit_bytes=40 * 2**20),
    )(gradients, errors, ortho, q)


def solution(mesh):
    in_specs = (P("dp", "tensor", None), P("dp", "tensor", None), P())
    out_specs = (P("dp", "tensor", None), P(), P("tensor", None))
    return jax.shard_map(
        per_device, mesh=mesh, in_specs=in_specs, out_specs=out_specs, check_vma=False
    )
```

```python
import functools

import jax
import jax.numpy as jnp
from jax import lax
from jax.experimental import pallas as pl
from jax.experimental.pallas import tpu as pltpu
from jax.sharding import PartitionSpec as P

MESH = pl.DeviceIdType.MESH
F32 = jnp.float32
BF16 = jnp.bfloat16
HIGHEST = lax.Precision.HIGHEST


def split3(x):
    hi = x.astype(BF16)
    rest = x - hi.astype(F32)
    mid = rest.astype(BF16)
    low = (rest - mid.astype(F32)).astype(BF16)
    return hi, mid, low


def eliminate(both, scale, first, last):
    rank = both.shape[0]
    rows = lax.broadcasted_iota(jnp.int32, (rank, 128), 0)
    for k in range(first, last):
        column = jnp.broadcast_to(both[:, k : k + 1], (rank, 128))
        pivot = column[k : k + 1, :]
        scale = jnp.where(rows == k, pivot, scale)
        factor = jnp.where(rows > k, column * (1.0 / pivot), 0.0)
        both = both - factor * both[k : k + 1, :]
    return both, scale


def reduce_kernel(
    n_dp, n_t, own_p, own_s,
    g_hbm, e_hbm, r_hbm, g_v, e_v, ortho_ref, q_ref,
    r_v, p_loc, p_in, p_full, s_acc, s_loc, s_in, z_in, q_full,
    gram_k, gram_in,
    g_sem, e_sem, r_sem,
    ps_send, ps_recv, pg_send, pg_recv, gr_send, gr_recv,
    ss_send, ss_recv, z_send, z_recv, q_send, q_recv,
):
    me = lax.axis_index("dp")
    mt = lax.axis_index("tensor")
    rank = r_v.shape[0]
    width = g_v.shape[1]
    cols = s_loc.shape[2]

    def peer(k):
        return lax.rem(me + k, n_dp)

    def tpeer(k):
        return lax.rem(mt + k, n_t)

    def chunk(d):
        return lax.rem(me + d, own_p)

    def remote(src, dst, send, recv, dp, t):
        return pltpu.make_async_remote_copy(
            src_ref=src, dst_ref=dst, send_sem=send, recv_sem=recv,
            device_id=(dp, t), device_id_type=MESH,
        )

    def guard(condition, always):
        if always:
            return lambda f: f()
        return pl.when(condition)

    def load(c):
        return (
            pltpu.make_async_copy(g_hbm.at[0, pl.ds(c * width, width)], g_v.at[c], g_sem.at[c]),
            pltpu.make_async_copy(e_hbm.at[0, pl.ds(c * width, width)], e_v.at[c], e_sem.at[c]),
        )

    r_copy = pltpu.make_async_copy(r_hbm, r_v, r_sem)
    r_copy.start()
    for d in range(1, own_p + 1):
        for copy in load(chunk(d)):
            copy.start()

    gram_k[...] = jnp.zeros_like(gram_k)
    barrier = pltpu.get_barrier_semaphore()
    for k in range(1, n_dp):
        pl.semaphore_signal(barrier, inc=1, device_id=(peer(k), mt), device_id_type=MESH)
    for k in range(1, n_t):
        pl.semaphore_signal(barrier, inc=1, device_id=(me, tpeer(k)), device_id_type=MESH)

    r_copy.wait()
    r3 = jnp.concatenate(split3(r_v[...]), axis=0)

    def fold(x):
        return x[:rank] + x[rank : 2 * rank] + x[2 * rank :]

    nt = (((1,), (1,)), ((), ()))

    for d in range(1, own_p + 1):
        c = chunk(d)
        for copy in load(c):
            copy.wait()
        both = lax.dot_general(r3, g_v[c], nt, preferred_element_type=F32)
        both += lax.dot_general(r3, e_v[c], nt, preferred_element_type=F32)
        p_loc[c] = fold(both)
        if d == 1:
            pl.semaphore_wait(barrier, n_dp - 1 + n_t - 1)
        if not (own_p == n_dp and d == own_p):
            @guard(c != me, own_p == n_dp)
            def _():
                remote(p_loc.at[c], p_in.at[me], ps_send.at[c], ps_recv.at[me], c, mt).start()

    is_p = me < own_p

    @guard(is_p, own_p == n_dp)
    def _():
        total = p_loc[me]
        for k in range(1, n_dp):
            o = peer(k)
            remote(p_loc.at[0], p_in.at[o], ps_send.at[0], ps_recv.at[o], o, mt).wait_recv()
            total = total + p_in[o]
        p_full[me] = total / n_dp
        for k in range(1, n_dp):
            o = peer(k)
            remote(p_full.at[me], p_full.at[me], pg_send.at[o], pg_recv.at[me], o, mt).start()

    for d in range(own_p):
        c = chunk(d)
        if not (own_p == n_dp and d == 0):
            @guard(c != me, own_p == n_dp)
            def _():
                remote(p_full.at[c], p_full.at[c], pg_send.at[0], pg_recv.at[c], c, mt).wait_recv()
        p = p_full[c]
        gram_k[c, :, :rank] = lax.dot_general(p, p, nt, precision=HIGHEST, preferred_element_type=F32)
        if d == own_p - 1:
            gram = gram_k[0]
            for k in range(1, own_p):
                gram = gram + gram_k[k]
            gram_in[mt] = gram
            for k in range(1, n_t):
                o = tpeer(k)
                remote(gram_in.at[mt], gram_in.at[mt], gr_send.at[o], gr_recv.at[mt], me, o).start()
        p3 = jnp.concatenate(split3(p), axis=0)
        both = jnp.dot(p3, g_v[c], preferred_element_type=F32)
        both += jnp.dot(p3, e_v[c], preferred_element_type=F32)
        if d == 0:
            s_acc[...] = fold(both)
        else:
            s_acc[...] += fold(both)

    for j in range(own_s):
        s_loc[j] = s_acc[:, j * cols : (j + 1) * cols]
    for d in range(1, own_s + 1):
        j = lax.rem(me + d, own_s)
        if not (own_s == n_dp and d == own_s):
            @guard(j != me, own_s == n_dp)
            def _():
                remote(s_loc.at[j], s_in.at[me], ss_send.at[j], ss_recv.at[me], j, mt).start()

    for k in range(1, n_t):
        o = tpeer(k)
        remote(gram_in.at[o], gram_in.at[o], gr_send.at[0], gr_recv.at[o], me, o).wait_recv()
    gram = gram_in[0]
    for k in range(1, n_t):
        gram = gram + gram_in[k]
    lanes = lax.broadcasted_iota(jnp.int32, (rank, 128), 1)
    rows = lax.broadcasted_iota(jnp.int32, (rank, 128), 0)
    gram = jnp.where(lanes < rank, gram, 0.0)
    both = jnp.where(lanes == rows + rank, 1.0, gram)
    scale = jnp.ones((rank, 128), F32)
    half = rank // 2
    is_s = me < own_s

    def share_sum():
        total = s_loc[me]
        for k in range(1, n_dp):
            o = peer(k)
            remote(s_loc.at[0], s_in.at[o], ss_send.at[0], ss_recv.at[o], o, mt).wait_recv()
            total = total + s_in[o]
        z_in[mt] = total
        for k in range(1, n_t):
            o = tpeer(k)
            remote(z_in.at[mt], z_in.at[mt], z_send.at[o], z_recv.at[mt], me, o).start()

    guard(is_s, own_s == n_dp)(share_sum)
    both, scale = eliminate(both, scale, 0, half)

    @guard(is_s, own_s == n_dp)
    def _():
        for k in range(1, n_t):
            o = tpeer(k)
            remote(z_in.at[o], z_in.at[o], z_send.at[0], z_recv.at[o], me, o).wait_recv()
        total = z_in[0]
        for k in range(1, n_t):
            total = total + z_in[k]
        q_full[me] = total / n_dp
        for k in range(1, n_dp):
            o = peer(k)
            remote(q_full.at[me], q_full.at[me], q_send.at[o], q_recv.at[me], o, mt).start()

    both, scale = eliminate(both, scale, half, rank)
    inverse = (both / jnp.sqrt(scale))[:, rank : 2 * rank]
    for c in range(own_p):
        ortho_ref[:, c * width : (c + 1) * width] = jnp.dot(
            inverse, p_full[c], precision=HIGHEST, preferred_element_type=F32
        )

    for d in range(1, own_s + 1):
        j = lax.rem(me + d, own_s)
        if not (own_s == n_dp and d == own_s):
            @guard(j != me, own_s == n_dp)
            def _():
                remote(q_full.at[j], q_full.at[j], q_send.at[0], q_recv.at[j], j, mt).wait_recv()
    for j in range(own_s):
        q_ref[:, j * cols : (j + 1) * cols] = jnp.dot(
            inverse, q_full[j], precision=HIGHEST, preferred_element_type=F32
        )

    for d in range(1, own_p + 1):
        c = chunk(d)
        if not (own_p == n_dp and d == own_p):
            @guard(c != me, own_p == n_dp)
            def _():
                remote(p_loc.at[c], p_in.at[me], ps_send.at[c], ps_recv.at[me], c, mt).wait_send()
    for d in range(1, own_s + 1):
        j = lax.rem(me + d, own_s)
        if not (own_s == n_dp and d == own_s):
            @guard(j != me, own_s == n_dp)
            def _():
                remote(s_loc.at[j], s_in.at[me], ss_send.at[j], ss_recv.at[me], j, mt).wait_send()
    for k in range(1, n_t):
        o = tpeer(k)
        remote(gram_in.at[mt], gram_in.at[mt], gr_send.at[o], gr_recv.at[mt], me, o).wait_send()

    @guard(is_p, own_p == n_dp)
    def _():
        for k in range(1, n_dp):
            o = peer(k)
            remote(p_full.at[me], p_full.at[me], pg_send.at[o], pg_recv.at[me], o, mt).wait_send()

    @guard(is_s, own_s == n_dp)
    def _():
        for k in range(1, n_dp):
            o = peer(k)
            remote(q_full.at[me], q_full.at[me], q_send.at[o], q_recv.at[me], o, mt).wait_send()
        for k in range(1, n_t):
            o = tpeer(k)
            remote(z_in.at[mt], z_in.at[mt], z_send.at[o], z_recv.at[mt], me, o).wait_send()


def apply_kernel(g_ref, e_ref, ortho_ref, q_ref, err_ref, factors_ref, update_ref, q6_ref):
    @pl.when(pl.program_id(0) == 0)
    def _():
        q = q_ref[...]
        factors_ref[...] = q
        hi, mid, low = split3(q)
        q6_ref[...] = jnp.concatenate([hi, mid, hi, low, mid, hi], axis=0)

    hi, mid, low = split3(ortho_ref[...])
    left = jnp.concatenate([hi, hi, mid, hi, mid, low], axis=0)
    approx = lax.dot_general(
        left, q6_ref[...], (((0,), (0,)), ((), ())), preferred_element_type=F32
    )
    update_ref[...] = approx.astype(BF16)
    err_ref[0] = ((g_ref[0].astype(F32) + e_ref[0].astype(F32)) - approx).astype(BF16)


def per_device(gradients, errors, right_factors):
    n_dp, n_t = lax.axis_size("dp"), lax.axis_size("tensor")
    rows, kv = gradients.shape[1:]
    rank = right_factors.shape[0]
    own_p = min(n_dp, rows // 128)
    own_s = min(n_dp, kv // 128)
    width, cols = rows // own_p, kv // own_s
    dma = pltpu.SemaphoreType.DMA
    held_g, held_e, ortho, q = pl.pallas_call(
        functools.partial(reduce_kernel, n_dp, n_t, own_p, own_s),
        out_shape=(
            pltpu.VMEM((own_p, width, kv), BF16),
            pltpu.VMEM((own_p, width, kv), BF16),
            pltpu.VMEM((rank, rows), F32),
            pltpu.VMEM((rank, kv), F32),
        ),
        in_specs=[pl.BlockSpec(memory_space=pl.ANY)] * 3,
        out_specs=(pl.BlockSpec(memory_space=pltpu.VMEM),) * 4,
        scratch_shapes=[
            pltpu.VMEM((rank, kv), F32),
            pltpu.VMEM((own_p, rank, width), F32),
            pltpu.VMEM((n_dp, rank, width), F32),
            pltpu.VMEM((own_p, rank, width), F32),
            pltpu.VMEM((rank, kv), F32),
            pltpu.VMEM((own_s, rank, cols), F32),
            pltpu.VMEM((n_dp, rank, cols), F32),
            pltpu.VMEM((n_t, rank, cols), F32),
            pltpu.VMEM((own_s, rank, cols), F32),
            pltpu.VMEM((own_p, rank, 128), F32),
            pltpu.VMEM((n_t, rank, 128), F32),
            dma((own_p,)), dma((own_p,)), dma,
            dma((own_p,)), dma((n_dp,)), dma((n_dp,)), dma((own_p,)),
            dma((n_t,)), dma((n_t,)),
            dma((own_s,)), dma((n_dp,)), dma((n_t,)), dma((n_t,)),
            dma((n_dp,)), dma((own_s,)),
        ],
        compiler_params=pltpu.CompilerParams(
            collective_id=0, has_side_effects=True, vmem_limit_bytes=51 * 2**20
        ),
    )(gradients, errors, right_factors)

    block = width
    held = pl.BlockSpec((1, block, kv), lambda i: (i, 0, 0))
    big = pl.BlockSpec((1, block, kv), lambda i: (0, i, 0))
    return pl.pallas_call(
        apply_kernel,
        grid=(rows // block,),
        out_shape=(
            jax.ShapeDtypeStruct((1, rows, kv), BF16),
            jax.ShapeDtypeStruct((rank, kv), F32),
            jax.ShapeDtypeStruct((rows, kv), BF16),
        ),
        in_specs=[
            held, held,
            pl.BlockSpec((rank, block), lambda i: (0, i)),
            pl.BlockSpec((rank, kv), lambda i: (0, 0)),
        ],
        out_specs=(
            big,
            pl.BlockSpec((rank, kv), lambda i: (0, 0)),
            pl.BlockSpec((block, kv), lambda i: (i, 0)),
        ),
        scratch_shapes=[pltpu.VMEM((6 * rank, kv), BF16)],
        compiler_params=pltpu.CompilerParams(vmem_limit_bytes=40 * 2**20),
    )(held_g, held_e, ortho, q)


def solution(mesh):
    in_specs = (P("dp", "tensor", None), P("dp", "tensor", None), P())
    out_specs = (P("dp", "tensor", None), P(), P("tensor", None))
    return jax.shard_map(
        per_device, mesh=mesh, in_specs=in_specs, out_specs=out_specs, check_vma=False
    )
```

```python
import functools

import jax
import jax.numpy as jnp
from jax import lax
from jax.experimental import pallas as pl
from jax.experimental.pallas import tpu as pltpu
from jax.sharding import PartitionSpec as P

MESH = pl.DeviceIdType.MESH
F32 = jnp.float32
BF16 = jnp.bfloat16
HIGHEST = lax.Precision.HIGHEST


def split3(x):
    hi = x.astype(BF16)
    rest = x - hi.astype(F32)
    mid = rest.astype(BF16)
    low = (rest - mid.astype(F32)).astype(BF16)
    return hi, mid, low


def eliminate(both, scale, first, last):
    rank = both.shape[0]
    rows = lax.broadcasted_iota(jnp.int32, (rank, 128), 0)
    for k in range(first, last):
        column = jnp.broadcast_to(both[:, k : k + 1], (rank, 128))
        pivot = column[k : k + 1, :]
        scale = jnp.where(rows == k, pivot, scale)
        factor = jnp.where(rows > k, column * (1.0 / pivot), 0.0)
        both = both - factor * both[k : k + 1, :]
    return both, scale


def reduce_kernel(
    n_dp, n_t, own_p, own_s,
    g_hbm, e_hbm, r_hbm, g_v, e_v, ortho_ref, q_ref,
    r_v, p_loc, p_in, p_full, s_acc, s_loc, s_in, z_in, q_full,
    gram_k, gram_in,
    g_sem, e_sem, r_sem,
    ps_send, ps_recv, pg_send, pg_recv, gr_send, gr_recv,
    ss_send, ss_recv, z_send, z_recv, q_send, q_recv,
):
    me = lax.axis_index("dp")
    mt = lax.axis_index("tensor")
    rank = r_v.shape[0]
    width = g_v.shape[1]
    cols = s_loc.shape[2]

    def peer(k):
        return lax.rem(me + k, n_dp)

    def tpeer(k):
        return lax.rem(mt + k, n_t)

    def chunk(d):
        return lax.rem(me + d, own_p)

    def remote(src, dst, send, recv, dp, t):
        return pltpu.make_async_remote_copy(
            src_ref=src, dst_ref=dst, send_sem=send, recv_sem=recv,
            device_id=(dp, t), device_id_type=MESH,
        )

    def guard(condition, always):
        if always:
            return lambda f: f()
        return pl.when(condition)

    def load(c):
        return (
            pltpu.make_async_copy(g_hbm.at[0, pl.ds(c * width, width)], g_v.at[c], g_sem.at[c]),
            pltpu.make_async_copy(e_hbm.at[0, pl.ds(c * width, width)], e_v.at[c], e_sem.at[c]),
        )

    r_copy = pltpu.make_async_copy(r_hbm, r_v, r_sem)
    r_copy.start()
    for d in range(1, own_p + 1):
        for copy in load(chunk(d)):
            copy.start()

    gram_k[...] = jnp.zeros_like(gram_k)
    barrier = pltpu.get_barrier_semaphore()
    for k in range(1, n_dp):
        pl.semaphore_signal(barrier, inc=1, device_id=(peer(k), mt), device_id_type=MESH)
    for k in range(1, n_t):
        pl.semaphore_signal(barrier, inc=1, device_id=(me, tpeer(k)), device_id_type=MESH)

    r_copy.wait()
    r3 = jnp.concatenate(split3(r_v[...]), axis=0)

    def fold(x):
        return x[:rank] + x[rank : 2 * rank] + x[2 * rank :]

    nt = (((1,), (1,)), ((), ()))

    for d in range(1, own_p + 1):
        c = chunk(d)
        for copy in load(c):
            copy.wait()
        both = lax.dot_general(r3, g_v[c], nt, preferred_element_type=F32)
        both += lax.dot_general(r3, e_v[c], nt, preferred_element_type=F32)
        p_loc[c] = fold(both)
        if d == 1:
            pl.semaphore_wait(barrier, n_dp - 1 + n_t - 1)
        if not (own_p == n_dp and d == own_p):
            @guard(c != me, own_p == n_dp)
            def _():
                remote(p_loc.at[c], p_in.at[me], ps_send.at[c], ps_recv.at[me], c, mt).start()

    is_p = me < own_p

    @guard(is_p, own_p == n_dp)
    def _():
        total = p_loc[me]
        for k in range(1, n_dp):
            o = peer(k)
            remote(p_loc.at[0], p_in.at[o], ps_send.at[0], ps_recv.at[o], o, mt).wait_recv()
            total = total + p_in[o]
        p_full[me] = total / n_dp
        for k in range(1, n_dp):
            o = peer(k)
            remote(p_full.at[me], p_full.at[me], pg_send.at[o], pg_recv.at[me], o, mt).start()

    for d in range(own_p):
        c = chunk(d)
        if not (own_p == n_dp and d == 0):
            @guard(c != me, own_p == n_dp)
            def _():
                remote(p_full.at[c], p_full.at[c], pg_send.at[0], pg_recv.at[c], c, mt).wait_recv()
        p = p_full[c]
        gram_k[c, :, :rank] = lax.dot_general(p, p, nt, precision=HIGHEST, preferred_element_type=F32)
        if d == own_p - 1:
            gram = gram_k[0]
            for k in range(1, own_p):
                gram = gram + gram_k[k]
            gram_in[mt] = gram
            for k in range(1, n_t):
                o = tpeer(k)
                remote(gram_in.at[mt], gram_in.at[mt], gr_send.at[o], gr_recv.at[mt], me, o).start()
        p3 = jnp.concatenate(split3(p), axis=0)
        both = jnp.dot(p3, g_v[c], preferred_element_type=F32)
        both += jnp.dot(p3, e_v[c], preferred_element_type=F32)
        if d == 0:
            s_acc[...] = fold(both)
        else:
            s_acc[...] += fold(both)

    for j in range(own_s):
        s_loc[j] = s_acc[:, j * cols : (j + 1) * cols]
    for d in range(1, own_s + 1):
        j = lax.rem(me + d, own_s)
        if not (own_s == n_dp and d == own_s):
            @guard(j != me, own_s == n_dp)
            def _():
                remote(s_loc.at[j], s_in.at[me], ss_send.at[j], ss_recv.at[me], j, mt).start()

    for k in range(1, n_t):
        o = tpeer(k)
        remote(gram_in.at[o], gram_in.at[o], gr_send.at[0], gr_recv.at[o], me, o).wait_recv()
    gram = gram_in[0]
    for k in range(1, n_t):
        gram = gram + gram_in[k]
    lanes = lax.broadcasted_iota(jnp.int32, (rank, 128), 1)
    rows = lax.broadcasted_iota(jnp.int32, (rank, 128), 0)
    gram = jnp.where(lanes < rank, gram, 0.0)
    both = jnp.where(lanes == rows + rank, 1.0, gram)
    scale = jnp.ones((rank, 128), F32)
    half = rank // 2
    is_s = me < own_s

    def share_sum():
        total = s_loc[me]
        for k in range(1, n_dp):
            o = peer(k)
            remote(s_loc.at[0], s_in.at[o], ss_send.at[0], ss_recv.at[o], o, mt).wait_recv()
            total = total + s_in[o]
        z_in[mt] = total
        for k in range(1, n_t):
            o = tpeer(k)
            remote(z_in.at[mt], z_in.at[mt], z_send.at[o], z_recv.at[mt], me, o).start()

    guard(is_s, own_s == n_dp)(share_sum)
    both, scale = eliminate(both, scale, 0, half)

    @guard(is_s, own_s == n_dp)
    def _():
        for k in range(1, n_t):
            o = tpeer(k)
            remote(z_in.at[o], z_in.at[o], z_send.at[0], z_recv.at[o], me, o).wait_recv()
        total = z_in[0]
        for k in range(1, n_t):
            total = total + z_in[k]
        q_full[me] = total / n_dp
        for k in range(1, n_dp):
            o = peer(k)
            remote(q_full.at[me], q_full.at[me], q_send.at[o], q_recv.at[me], o, mt).start()

    both, scale = eliminate(both, scale, half, rank)
    inverse = (both / jnp.sqrt(scale))[:, rank : 2 * rank]
    for c in range(own_p):
        ortho_ref[:, c * width : (c + 1) * width] = jnp.dot(
            inverse, p_full[c], precision=HIGHEST, preferred_element_type=F32
        )

    for d in range(1, own_s + 1):
        j = lax.rem(me + d, own_s)
        if not (own_s == n_dp and d == own_s):
            @guard(j != me, own_s == n_dp)
            def _():
                remote(q_full.at[j], q_full.at[j], q_send.at[0], q_recv.at[j], j, mt).wait_recv()
    for j in range(own_s):
        q_ref[:, j * cols : (j + 1) * cols] = jnp.dot(
            inverse, q_full[j], precision=HIGHEST, preferred_element_type=F32
        )

    for d in range(1, own_p + 1):
        c = chunk(d)
        if not (own_p == n_dp and d == own_p):
            @guard(c != me, own_p == n_dp)
            def _():
                remote(p_loc.at[c], p_in.at[me], ps_send.at[c], ps_recv.at[me], c, mt).wait_send()
    for d in range(1, own_s + 1):
        j = lax.rem(me + d, own_s)
        if not (own_s == n_dp and d == own_s):
            @guard(j != me, own_s == n_dp)
            def _():
                remote(s_loc.at[j], s_in.at[me], ss_send.at[j], ss_recv.at[me], j, mt).wait_send()
    for k in range(1, n_t):
        o = tpeer(k)
        remote(gram_in.at[mt], gram_in.at[mt], gr_send.at[o], gr_recv.at[mt], me, o).wait_send()

    @guard(is_p, own_p == n_dp)
    def _():
        for k in range(1, n_dp):
            o = peer(k)
            remote(p_full.at[me], p_full.at[me], pg_send.at[o], pg_recv.at[me], o, mt).wait_send()

    @guard(is_s, own_s == n_dp)
    def _():
        for k in range(1, n_dp):
            o = peer(k)
            remote(q_full.at[me], q_full.at[me], q_send.at[o], q_recv.at[me], o, mt).wait_send()
        for k in range(1, n_t):
            o = tpeer(k)
            remote(z_in.at[mt], z_in.at[mt], z_send.at[o], z_recv.at[mt], me, o).wait_send()


def apply_kernel(g_ref, e_ref, ortho_ref, q_ref, err_ref, factors_ref, update_ref, q6_ref):
    @pl.when(pl.program_id(0) == 0)
    def _():
        q = q_ref[...]
        factors_ref[...] = q
        hi, mid, low = split3(q)
        q6_ref[...] = jnp.concatenate([hi, mid, hi, low, mid, hi], axis=0)

    hi, mid, low = split3(ortho_ref[...])
    left = jnp.concatenate([hi, hi, mid, hi, mid, low], axis=0)
    approx = lax.dot_general(
        left, q6_ref[...], (((0,), (0,)), ((), ())), preferred_element_type=F32
    )
    update_ref[...] = approx.astype(BF16)
    merged = g_ref[...].astype(F32) + e_ref[...].astype(F32)
    err_ref[0] = (merged.reshape(approx.shape) - approx).astype(BF16)


def per_device(gradients, errors, right_factors):
    n_dp, n_t = lax.axis_size("dp"), lax.axis_size("tensor")
    rows, kv = gradients.shape[1:]
    rank = right_factors.shape[0]
    own_p = min(n_dp, rows // 128)
    own_s = min(n_dp, kv // 128)
    width, cols = rows // own_p, kv // own_s
    dma = pltpu.SemaphoreType.DMA
    held_g, held_e, ortho, q = pl.pallas_call(
        functools.partial(reduce_kernel, n_dp, n_t, own_p, own_s),
        out_shape=(
            pltpu.VMEM((own_p, width, kv), BF16),
            pltpu.VMEM((own_p, width, kv), BF16),
            pltpu.VMEM((rank, rows), F32),
            pltpu.VMEM((rank, kv), F32),
        ),
        in_specs=[pl.BlockSpec(memory_space=pl.ANY)] * 3,
        out_specs=(pl.BlockSpec(memory_space=pltpu.VMEM),) * 4,
        scratch_shapes=[
            pltpu.VMEM((rank, kv), F32),
            pltpu.VMEM((own_p, rank, width), F32),
            pltpu.VMEM((n_dp, rank, width), F32),
            pltpu.VMEM((own_p, rank, width), F32),
            pltpu.VMEM((rank, kv), F32),
            pltpu.VMEM((own_s, rank, cols), F32),
            pltpu.VMEM((n_dp, rank, cols), F32),
            pltpu.VMEM((n_t, rank, cols), F32),
            pltpu.VMEM((own_s, rank, cols), F32),
            pltpu.VMEM((own_p, rank, 128), F32),
            pltpu.VMEM((n_t, rank, 128), F32),
            dma((own_p,)), dma((own_p,)), dma,
            dma((own_p,)), dma((n_dp,)), dma((n_dp,)), dma((own_p,)),
            dma((n_t,)), dma((n_t,)),
            dma((own_s,)), dma((n_dp,)), dma((n_t,)), dma((n_t,)),
            dma((n_dp,)), dma((own_s,)),
        ],
        compiler_params=pltpu.CompilerParams(
            collective_id=0, has_side_effects=True, vmem_limit_bytes=51 * 2**20
        ),
    )(gradients, errors, right_factors)

    per = 2 if own_p % 2 == 0 else 1
    block = per * width
    held = pl.BlockSpec((per, width, kv), lambda i: (i, 0, 0))
    big = pl.BlockSpec((1, block, kv), lambda i: (0, i, 0))
    return pl.pallas_call(
        apply_kernel,
        grid=(rows // block,),
        out_shape=(
            jax.ShapeDtypeStruct((1, rows, kv), BF16),
            jax.ShapeDtypeStruct((rank, kv), F32),
            jax.ShapeDtypeStruct((rows, kv), BF16),
        ),
        in_specs=[
            held, held,
            pl.BlockSpec((rank, block), lambda i: (0, i)),
            pl.BlockSpec((rank, kv), lambda i: (0, 0)),
        ],
        out_specs=(
            big,
            pl.BlockSpec((rank, kv), lambda i: (0, 0)),
            pl.BlockSpec((block, kv), lambda i: (i, 0)),
        ),
        scratch_shapes=[pltpu.VMEM((6 * rank, kv), BF16)],
        compiler_params=pltpu.CompilerParams(vmem_limit_bytes=40 * 2**20),
    )(held_g, held_e, ortho, q)


def solution(mesh):
    in_specs = (P("dp", "tensor", None), P("dp", "tensor", None), P())
    out_specs = (P("dp", "tensor", None), P(), P("tensor", None))
    return jax.shard_map(
        per_device, mesh=mesh, in_specs=in_specs, out_specs=out_specs, check_vma=False
    )
```
